32 devices in a mesh: groups: 2 (over x), node: 8 (over z, core), local: 2 (over y).
Axes of the slice: x: 2, y: 2, z: 4, core: 2. Of those that a mesh axis runs over, the one named last changes fastest.
Arguments:
- tokens: bfloat16 [128, 3584], P(('groups', 'node', 'local')), parts along dimension 0, may hold values from -6 to 6
- node_ids: int32 [128, 4], P(('groups', 'node', 'local')), parts along dimension 0, may hold values from 0 to 7, all different within a row; in each aligned block of 4 rows (0 to 3, 4 to 7, ...) at most 4 rows name the same one
- expert_order: int32 [128, 4, 3], P(('groups', 'node', 'local')), parts along dimension 0, may hold values from 0 to 2, each once within a row
- gate_weights: bfloat16 [128, 4, 2], P(('groups', 'node', 'local')), parts along dimension 0, may hold values from 0.049804688 to 0.59765625
- expert_gate: bfloat16 [24, 3584, 1024], P('node', None, 'local'), may hold values from -0.09375 to 0.09375
- expert_up: bfloat16 [24, 3584, 1024], P('node', None, 'local'), may hold values from -0.09375 to 0.09375
- expert_down: bfloat16 [24, 1024, 3584], P('node', 'local'), may hold values from -0.1875 to 0.1875
- shared_gate: bfloat16 [3584, 1024], P(None, 'local'), may hold values from -0.09375 to 0.09375
- shared_up: bfloat16 [3584, 1024], P(None, 'local'), may hold values from -0.09375 to 0.09375
- shared_down: bfloat16 [1024, 3584], P('local'), may hold values from -0.1875 to 0.1875
Outputs:
- layer_output: bfloat16 [128, 3584], P(('groups', 'node', 'local')), parts along dimension 0
The draws below stay inside these ranges and needn't reach their ends.
There are 2 independent parts, one for each index of `groups`. The reference program is written for one: setup_inputs(seed, part) draws one part's arguments, and reference() takes and returns one part's arrays. A program takes and returns all parts, laid end to end along the dimension named above; an argument that names none is the same for every part. Nothing has to cross between parts.
Inputs may be any that keep to these rules, and one draw needn't show every extreme that they name: `node_ids`: each row names 4 different nodes. Among the rows of one device no node is named by more than 4 rows, and in every draw some device names some node exactly 4 times. `expert_order`: for each row and each of its nodes, the 3 entries are a permutation of 0 to 2.
All inputs are finite; a program needn't handle non-finite values.
Results may differ from the reference program's by a relative error of at most 0.008.
Values may be sent and summed in bfloat16 or wider, within the bound.
A program may use at most 128 MiB of HBM per device.

```python
import math
import jax
import jax.numpy as jnp
import numpy as np
from jax import lax

D = 3584
F_EXP = 1024
F_SH = 1024
E_NODE = 3
NODE_TOP = 4
PICK = 2
TOK_DEV = 4
TOKENS = 64
EXPERTS = 24
CAP = 4
N_NODE = 8
N_LOCAL = 2


def shard_levels(own_key, shape, split, least, top_value):
    factor_of, own = 1.0, jax.random.fold_in(own_key, 6)
    for axis_at, parts in split:
        heights = jnp.exp(jax.random.uniform(jax.random.fold_in(own, axis_at), (parts,), jnp.float32, least / len(split), top_value / len(split)))
        factor_of = factor_of * jnp.repeat(heights, shape[axis_at] // parts).reshape([-1 if axis == axis_at else 1 for axis in range(len(shape))])
    return factor_of


def assign_block(rng, own, number, rows, count, top, bound, lean):
    sequence = jax.random.permutation(rng, count)
    heavy_load, usual = load_shares(count, rows * top, bound, lean, True), load_shares(count, rows * top, bound, lean, False)
    places = jnp.arange(count)

    def named(lengths, turn):
        used = int((lengths > 0).sum())
        fixed = max(1, used // 4)
        passed = fixed + (places - fixed + turn * (used - fixed)) % max(1, count - fixed)
        return jnp.zeros((count,), jnp.int32).at[sequence[jnp.where(places < fixed, places, passed)]].set(jnp.asarray(lengths, jnp.int32))

    lengths = jnp.where(number % 4 == 0, named(heavy_load, number // 4), named(usual, number - number // 4 - 1))
    mixed = jax.random.permutation(jax.random.fold_in(own, 3), count)
    source_of, receiver = mixed[0:count // 2 * 2:2], mixed[1:count // 2 * 2:2]
    room = jnp.minimum(lengths[source_of] - 1, bound - lengths[receiver]) // 2
    room = jnp.where((source_of == sequence[0]) | (receiver == sequence[0]) | (lengths[receiver] == 0), 0, jnp.maximum(room, 0))
    passed = jax.random.randint(jax.random.fold_in(own, 4), (count // 2,), 0, 1 << 20) % (room + 1)
    lengths = lengths.at[source_of].add(-passed).at[receiver].add(passed)
    members = jnp.searchsorted(jnp.cumsum(lengths), jnp.arange(rows * top), side="right").astype(jnp.int32)
    table = members.reshape(top, rows).T
    table = table[jax.random.permutation(jax.random.fold_in(own, 1), rows)]
    turn = jax.random.randint(jax.random.fold_in(own, 2), (rows, 1), 0, top)
    return jnp.take_along_axis(table, (jnp.arange(top)[None, :] + turn) % top, axis=1)


def load_shares(amount, total, most, lean, full):
    weights = [(1 << 20) // math.isqrt(standing ** lean) + 1 for standing in range(1, amount + 1)]
    largest = most if full else min(most, max(-(-total // amount), total * weights[0] // sum(weights)))
    least = 1 if total - largest >= amount - 1 else 0
    given, surplus = [largest] + [least] * (amount - 1), total - largest - least * (amount - 1)
    while surplus > 0:
        candidates = [i for i in range(1, amount) if given[i] < largest] or [i for i in range(1, amount) if given[i] < most]
        mass, budget = sum([weights[i] for i in candidates]), surplus
        for i in candidates:
            more = min(most - given[i], max(1, budget * weights[i] // mass), surplus)
            given[i] = given[i] + more
            surplus = surplus - more
    return np.array(given)


def centred(key, shape, scale, most, pieces=(), kind=jnp.bfloat16):
    gain = shard_levels(key, shape, pieces, -0.22, 0.18) if pieces else 1.0
    values = jax.random.normal(key, shape, jnp.float32) * scale * gain
    return jnp.minimum(jnp.maximum(values, -most), most).astype(kind)


def setup_inputs(seed: int = 0, part: int = 0) -> dict:
    splits = jax.random.split(jax.random.key(seed), 11)
    part_splits = jax.random.split(jax.random.fold_in(splits[10], part), 11)
    tokens = centred(part_splits[0], (TOKENS, D), 1.0, 6.0, ((0, 16),))
    node_ids_keys = jax.random.split(jax.random.fold_in(part_splits[1], 1), TOKENS // TOK_DEV)
    node_ids_turns = jax.random.permutation(jax.random.fold_in(part_splits[1], 3), TOKENS // TOK_DEV)
    node_ids = jax.vmap(lambda own, number: assign_block(jax.random.fold_in(part_splits[1], 2), own, number, TOK_DEV, N_NODE, NODE_TOP, CAP, 2))(node_ids_keys, node_ids_turns).reshape((TOKENS, NODE_TOP))
    expert_order = jax.vmap(lambda own: jax.random.permutation(own, E_NODE))(jax.random.split(part_splits[2], TOKENS * NODE_TOP)).reshape((TOKENS, NODE_TOP, E_NODE)).astype(jnp.int32)
    gate_weights = jnp.clip(jnp.exp(math.log(0.59765625) - 2.4849066 * jax.random.uniform(part_splits[3], (TOKENS, NODE_TOP, PICK), jnp.float32) ** shard_levels(part_splits[3], (TOKENS, NODE_TOP, PICK), ((0, 16),), -0.2, 0.2)), 0.049804688, 0.59765625).astype(jnp.bfloat16)
    expert_gate = centred(splits[4], (EXPERTS, D, F_EXP), D ** -0.5, 0.09375, ((0, 8), (2, 2)))
    expert_up = centred(splits[5], (EXPERTS, D, F_EXP), D ** -0.5, 0.09375, ((0, 8), (2, 2)))
    expert_down = centred(splits[6], (EXPERTS, F_EXP, D), F_EXP ** -0.5, 0.1875, ((0, 8), (1, 2)))
    shared_gate = centred(splits[7], (D, F_SH), D ** -0.5, 0.09375, ((1, 2),))
    shared_up = centred(splits[8], (D, F_SH), D ** -0.5, 0.09375, ((1, 2),))
    shared_down = centred(splits[9], (F_SH, D), F_SH ** -0.5, 0.1875, ((0, 2),))
    return {"tokens": tokens, "node_ids": node_ids, "expert_order": expert_order, "gate_weights": gate_weights, "expert_gate": expert_gate, "expert_up": expert_up, "expert_down": expert_down, "shared_gate": shared_gate, "shared_up": shared_up, "shared_down": shared_down}


def expert_sum(buffer, gate_buffer, w_gate, w_up, w_down):
    rows_wide = buffer.astype(jnp.float32)
    gate_part = jnp.einsum("md,edf->mef", rows_wide, w_gate.astype(jnp.float32), precision=lax.Precision.HIGHEST)
    up_part = jnp.einsum("md,edf->mef", rows_wide, w_up.astype(jnp.float32), precision=lax.Precision.HIGHEST)
    hidden = (jax.nn.silu(gate_part) * up_part * gate_buffer.astype(jnp.float32)[:, :, None]).astype(jnp.bfloat16)
    block_width = hidden.shape[2] // N_LOCAL
    running = jnp.zeros((buffer.shape[0], w_down.shape[2]), jnp.float32)
    for block_index in range(N_LOCAL):
        first_unit = block_index * block_width
        block_term = jnp.einsum("mef,efd->md", hidden[:, :, first_unit:first_unit + block_width].astype(jnp.float32), w_down[:, first_unit:first_unit + block_width, :].astype(jnp.float32), precision=lax.Precision.HIGHEST)
        block_term = lax.optimization_barrier(block_term.astype(jnp.bfloat16))
        running = running + block_term.astype(jnp.float32)
    return running


def reference(tokens, node_ids, expert_order, gate_weights, expert_gate, expert_up, expert_down, shared_gate, shared_up, shared_down):
    row_total = tokens.shape[0]
    devices = N_NODE * N_LOCAL
    slot_total = devices * CAP
    node_hit = node_ids[:, :, None] == jnp.arange(N_NODE, dtype=jnp.int32)[None, None, :]
    sent_mask = jnp.any(node_hit, axis=1)
    sent_count = sent_mask.astype(jnp.int32).reshape(devices, TOK_DEV, N_NODE)
    earlier = (jnp.cumsum(sent_count, axis=1) - sent_count).reshape(row_total, N_NODE).astype(jnp.int32)
    source = (jnp.arange(row_total, dtype=jnp.int32) // TOK_DEV).astype(jnp.int32)
    slot_index = jnp.where(sent_mask, source[:, None] * CAP + earlier, slot_total).astype(jnp.int32)
    pick_hit = (expert_order[:, :, :PICK, None] == jnp.arange(E_NODE, dtype=jnp.int32)[None, None, None, :]).astype(jnp.float32)
    node_gate = jnp.sum(pick_hit * gate_weights.astype(jnp.float32)[:, :, :, None], axis=2)
    gate_to_node = jnp.einsum("tkn,tke->tne", node_hit.astype(jnp.float32), node_gate, precision=lax.Precision.HIGHEST)
    width = tokens.shape[1]

    def one_node(running, inputs):
        w_gate, w_up, w_down, slot_where, node_gates = inputs
        buffer = jnp.zeros((slot_total, width), tokens.dtype).at[slot_where].set(tokens, mode="drop")
        gate_buffer = jnp.zeros((slot_total, E_NODE), jnp.bfloat16).at[slot_where].set(node_gates.astype(jnp.bfloat16), mode="drop")
        result = expert_sum(buffer, gate_buffer, w_gate, w_up, w_down).astype(jnp.bfloat16)
        node_back = jnp.take(result, slot_where, axis=0, mode="fill", fill_value=0)
        return running + node_back.astype(jnp.float32), None

    stacked = (expert_gate.reshape(N_NODE, E_NODE, width, F_EXP), expert_up.reshape(N_NODE, E_NODE, width, F_EXP), expert_down.reshape(N_NODE, E_NODE, F_EXP, width), slot_index.T, jnp.transpose(gate_to_node, (1, 0, 2)))
    routed, _ = lax.scan(one_node, jnp.zeros((row_total, width), jnp.float32), stacked)
    shared_g = jnp.dot(tokens, shared_gate, preferred_element_type=jnp.float32)
    shared_u = jnp.dot(tokens, shared_up, preferred_element_type=jnp.float32)
    shared_hidden = (jax.nn.silu(shared_g) * shared_u).astype(jnp.bfloat16)
    block_width = F_SH // N_LOCAL
    shared_sum = jnp.zeros((row_total, width), jnp.float32)
    for block_index in range(N_LOCAL):
        first_unit = block_index * block_width
        block_term = jnp.dot(shared_hidden[:, first_unit:first_unit + block_width], shared_down[first_unit:first_unit + block_width, :], preferred_element_type=jnp.float32)
        block_term = lax.optimization_barrier(block_term.astype(jnp.bfloat16))
        shared_sum = shared_sum + block_term.astype(jnp.float32)
    return (routed + shared_sum).astype(jnp.bfloat16)
```

```python
import functools

import jax
import jax.numpy as jnp
from jax import lax
from jax.experimental import pallas as pl
from jax.experimental.pallas import tpu as pltpu
from jax.sharding import PartitionSpec as P

MESH = pl.DeviceIdType.MESH
LANES = 128
CHUNKS = 4


def layer_kernel(
    nodes,
    locals_,
    packed,
    w_gate,
    w_up,
    w_down,
    s_gate,
    s_up,
    s_down,
    out,
    gate_v,
    up_v,
    sgate_v,
    sup_v,
    down_v,
    gathered,
    rows_wide,
    rows,
    hidden,
    sib_out,
    sib_in,
    mine,
    piece_out,
    piece_in,
    gate_sem,
    up_sem,
    sg_sem,
    su_sem,
    down_sem,
    g_send,
    g_recv,
    f_send,
    f_recv,
    s_send,
    s_recv,
    b_send,
    b_recv,
):
    experts, width, units = w_gate.shape
    row_count = packed.shape[0]
    chunks, _, chunk = down_v.shape
    peers = (nodes // 2) * locals_
    node = lax.axis_index("node")
    local = lax.axis_index("local")
    core = lax.rem(node, 2)
    my_peer = (node // 2) * locals_ + local

    def peer_id(peer, parity):
        return {"node": 2 * (peer // locals_) + parity, "local": lax.rem(peer, locals_)}

    def place(peer, parity):
        return (2 * (peer // locals_) + parity) * locals_ + lax.rem(peer, locals_)

    sibling = {"node": node + 1 - 2 * core, "local": local}

    blocks = s_gate.shape[1] // LANES
    share = nodes // blocks
    block_start = pl.multiple_of((node // share) * LANES, LANES)
    loads = []
    for e in range(experts):
        loads.append(pltpu.make_async_copy(w_gate.at[e], gate_v.at[e], gate_sem.at[e]))
        loads.append(pltpu.make_async_copy(w_up.at[e], up_v.at[e], up_sem.at[e]))
    sg_load = pltpu.make_async_copy(s_gate.at[:, pl.ds(block_start, LANES)], sgate_v, sg_sem)
    su_load = pltpu.make_async_copy(s_up.at[:, pl.ds(block_start, LANES)], sup_v, su_sem)
    loads += [sg_load, su_load]
    down_loads = []
    for c in range(chunks):
        cols = pl.ds(c * chunk, chunk)
        group = [
            pltpu.make_async_copy(
                w_down.at[e, :, cols],
                down_v.at[c, pl.ds(e * units, units), :],
                down_sem.at[c, e],
            )
            for e in range(experts)
        ]
        group.append(
            pltpu.make_async_copy(
                s_down.at[pl.ds(block_start, LANES), cols],
                down_v.at[c, pl.ds(experts * units, LANES), :],
                down_sem.at[c, experts],
            )
        )
        down_loads.append(group)
        loads += group
    for load in loads:
        load.start()

    barrier = pltpu.get_barrier_semaphore()
    pl.semaphore_signal(barrier, inc=1, device_id=sibling, device_id_type=MESH)

    def greet(step, carry):
        peer = lax.rem(my_peer + step, peers)
        pl.semaphore_signal(barrier, inc=1, device_id=peer_id(peer, core), device_id_type=MESH)
        return carry

    lax.fori_loop(1, peers, greet, 0)
    pl.semaphore_wait(barrier, peers)

    def gather_copy(step):
        return pltpu.make_async_remote_copy(
            src_ref=packed,
            dst_ref=gathered.at[place(my_peer, core)],
            send_sem=g_send.at[step],
            recv_sem=g_recv.at[step],
            device_id=peer_id(lax.rem(my_peer + step, peers), core),
            device_id_type=MESH,
        )

    def forward_copy(step):
        where = place(lax.rem(my_peer - step + peers, peers), core)
        return pltpu.make_async_remote_copy(
            src_ref=gathered.at[where],
            dst_ref=gathered.at[where],
            send_sem=f_send.at[step],
            recv_sem=f_recv.at[step],
            device_id=sibling,
            device_id_type=MESH,
        )

    own_forward = pltpu.make_async_remote_copy(
        src_ref=packed,
        dst_ref=gathered.at[place(my_peer, core)],
        send_sem=f_send.at[0],
        recv_sem=f_recv.at[0],
        device_id=sibling,
        device_id_type=MESH,
    )

    def start_gather(step, carry):
        gather_copy(step).start()
        return carry

    lax.fori_loop(1, peers, start_gather, 0)
    own_forward.start()
    gathered[place(my_peer, core)] = packed[...]

    def pass_on(step, carry):
        gather_copy(step).wait_recv()
        forward_copy(step).start()
        return carry

    lax.fori_loop(1, peers, pass_on, 0)

    def arrived(step, carry):
        forward_copy(step).wait_recv()
        return carry

    lax.fori_loop(0, peers, arrived, 0)
    for i in range(nodes * locals_):
        rows_wide[i * row_count : (i + 1) * row_count, :] = gathered[i].astype(jnp.float32)
    rows[...] = rows_wide[:, :width].astype(jnp.bfloat16)

    gates = rows_wide[:, width:]
    lane = lax.broadcasted_iota(jnp.int32, gates.shape, 1)

    def expert(e, carry):
        pltpu.make_async_copy(w_gate.at[e], gate_v.at[e], gate_sem.at[e]).wait()
        g = jnp.dot(rows[...], gate_v[e], preferred_element_type=jnp.float32)
        pltpu.make_async_copy(w_up.at[e], up_v.at[e], up_sem.at[e]).wait()
        u = jnp.dot(rows[...], up_v[e], preferred_element_type=jnp.float32)
        weight = jnp.sum(jnp.where(lane == node * experts + e, gates, 0.0), axis=1, keepdims=True)
        value = g / (1.0 + jnp.exp(-g)) * u * weight
        hidden[:, pl.ds(pl.multiple_of(e * units, LANES), units)] = value.astype(jnp.bfloat16)
        return carry

    lax.fori_loop(0, experts, expert, 0)
    sg_load.wait()
    g = jnp.dot(rows[...], sgate_v[...], preferred_element_type=jnp.float32)
    su_load.wait()
    u = jnp.dot(rows[...], sup_v[...], preferred_element_type=jnp.float32)
    part = LANES // share
    first = lax.rem(node, share) * part
    unit = lax.broadcasted_iota(jnp.int32, g.shape, 1)
    owned = jnp.logical_and(unit >= first, unit < first + part)
    value = jnp.where(owned, g / (1.0 + jnp.exp(-g)) * u, 0.0)
    hidden[:, experts * units :] = value.astype(jnp.bfloat16)

    def sib_copy(c):
        return pltpu.make_async_remote_copy(
            src_ref=sib_out.at[c],
            dst_ref=sib_in.at[c],
            send_sem=s_send.at[c],
            recv_sem=s_recv.at[c],
            device_id=sibling,
            device_id_type=MESH,
        )

    def piece_copy(c, step):
        peer = lax.rem(my_peer + step, peers)
        return pltpu.make_async_remote_copy(
            src_ref=piece_out.at[c, peer],
            dst_ref=piece_in.at[c, step],
            send_sem=b_send.at[c, step],
            recv_sem=b_recv.at[c, step],
            device_id=peer_id(peer, core),
            device_id_type=MESH,
        )

    span = locals_ * row_count

    def project(c):
        for load in down_loads[c]:
            load.wait()
        total = jnp.dot(hidden[...], down_v[c], preferred_element_type=jnp.float32)
        for z in range(nodes // 2):
            even = total[2 * z * span : (2 * z + 1) * span]
            odd = total[(2 * z + 1) * span : (2 * z + 2) * span]
            mine[c, z * span : (z + 1) * span, :] = jnp.where(core == 0, even, odd)
            sib_out[c, z * span : (z + 1) * span, :] = jnp.where(core == 0, odd, even).astype(
                jnp.bfloat16
            )
        sib_copy(c).start()

    def send_on(c):
        sib_copy(c).wait_recv()
        both = (mine[c] + sib_in[c].astype(jnp.float32)).astype(jnp.bfloat16)
        for peer in range(peers):
            piece_out[c, peer] = both[peer * row_count : (peer + 1) * row_count]

        def start_piece(step, carry):
            piece_copy(c, step).start()
            return carry

        lax.fori_loop(1, peers, start_piece, 0)

    def finish(c):
        def add(step, total):
            piece_copy(c, step).wait_recv()
            return total + piece_in[c, step].astype(jnp.float32)

        total = lax.fori_loop(1, peers, add, piece_out[c, my_peer].astype(jnp.float32))
        out[:, c * chunk : (c + 1) * chunk] = total.astype(jnp.bfloat16)

    for c in range(chunks):
        project(c)
        if c >= 1:
            send_on(c - 1)
    send_on(chunks - 1)
    for c in range(chunks):
        finish(c)

    own_forward.wait_send()

    def sent(step, carry):
        gather_copy(step).wait_send()
        forward_copy(step).wait_send()
        for c in range(chunks):
            piece_copy(c, step).wait_send()
        return carry

    lax.fori_loop(1, peers, sent, 0)
    for c in range(chunks):
        sib_copy(c).wait_send()


def per_device(
    nodes,
    locals_,
    tokens,
    node_ids,
    expert_order,
    gate_weights,
    expert_gate,
    expert_up,
    expert_down,
    shared_gate,
    shared_up,
    shared_down,
):
    row_count, width = tokens.shape
    experts, _, units = expert_gate.shape
    pick = gate_weights.shape[2]
    gate_lanes = -(-nodes * experts // LANES) * LANES
    target = node_ids[:, :, None] * experts + expert_order[:, :, :pick]
    hit = target[:, :, :, None] == jnp.arange(gate_lanes, dtype=jnp.int32)
    gates = jnp.sum(
        jnp.where(hit, gate_weights.astype(jnp.float32)[:, :, :, None], 0.0), axis=(1, 2)
    ).astype(jnp.bfloat16)
    packed = jnp.concatenate([tokens, gates], axis=1)
    full = width + gate_lanes
    devices = nodes * locals_
    peers = devices // 2
    total = devices * row_count
    chunk = width // CHUNKS
    deep = experts * units + LANES
    half = total // 2
    bf, f32 = jnp.bfloat16, jnp.float32
    dma = pltpu.SemaphoreType.DMA
    hbm = pl.BlockSpec(memory_space=pl.ANY)
    vmem = pl.BlockSpec(memory_space=pltpu.VMEM)
    return pl.pallas_call(
        functools.partial(layer_kernel, nodes, locals_),
        out_shape=jax.ShapeDtypeStruct((row_count, width), bf),
        in_specs=[vmem] + [hbm] * 6,
        out_specs=vmem,
        scratch_shapes=[
            pltpu.VMEM((experts, width, units), bf),
            pltpu.VMEM((experts, width, units), bf),
            pltpu.VMEM((width, LANES), bf),
            pltpu.VMEM((width, LANES), bf),
            pltpu.VMEM((CHUNKS, deep, chunk), bf),
            pltpu.VMEM((devices, row_count, full), bf),
            pltpu.VMEM((total, full), f32),
            pltpu.VMEM((total, width), bf),
            pltpu.VMEM((total, deep), bf),
            pltpu.VMEM((CHUNKS, half, chunk), bf),
            pltpu.VMEM((CHUNKS, half, chunk), bf),
            pltpu.VMEM((CHUNKS, half, chunk), f32),
            pltpu.VMEM((CHUNKS, peers, row_count, chunk), bf),
            pltpu.VMEM((CHUNKS, peers, row_count, chunk), bf),
            dma((experts,)),
            dma((experts,)),
            dma,
            dma,
            dma((CHUNKS, experts + 1)),
            dma((peers,)),
            dma((peers,)),
            dma((peers,)),
            dma((peers,)),
            dma((CHUNKS,)),
            dma((CHUNKS,)),
            dma((CHUNKS, peers)),
            dma((CHUNKS, peers)),
        ],
        compiler_params=pltpu.CompilerParams(
            collective_id=0, has_side_effects=True, vmem_limit_bytes=60 * 2**20
        ),
        cost_estimate=pl.CostEstimate(
            flops=6 * total * width * deep,
            bytes_accessed=6 * width * deep,
            transcendentals=total * deep,
        ),
    )(packed, expert_gate, expert_up, expert_down, shared_gate, shared_up, shared_down)


def solution(mesh):
    return jax.shard_map(
        functools.partial(per_device, mesh.shape["node"], mesh.shape["local"]),
        mesh=mesh,
        in_specs=(
            P(("groups", "node", "local"), None),
            P(("groups", "node", "local"), None),
            P(("groups", "node", "local"), None, None),
            P(("groups", "node", "local"), None, None),
            P("node", None, "local"),
            P("node", None, "local"),
            P("node", "local", None),
            P(None, "local"),
            P(None, "local"),
            P("local", None),
        ),
        out_specs=P(("groups", "node", "local"), None),
        check_vma=False,
    )
```

```python
import functools

import jax
import jax.numpy as jnp
from jax import lax
from jax.experimental import pallas as pl
from jax.experimental.pallas import tpu as pltpu
from jax.sharding import PartitionSpec as P

MESH = pl.DeviceIdType.MESH
LANES = 128
CHUNKS = 4


def layer_kernel(
    nodes,
    locals_,
    tokens,
    node_ids,
    expert_order,
    gate_weights,
    w_gate,
    w_up,
    w_down,
    s_gate,
    s_up,
    s_down,
    out,
    gate_v,
    up_v,
    sgate_v,
    sup_v,
    down_v,
    packed,
    gathered,
    rows_wide,
    rows,
    hidden,
    sib_out,
    sib_in,
    mine,
    piece_out,
    piece_in,
    gate_sem,
    up_sem,
    sg_sem,
    su_sem,
    down_sem,
    g_send,
    g_recv,
    f_send,
    f_recv,
    s_send,
    s_recv,
    b_send,
    b_recv,
):
    experts, width, units = w_gate.shape
    row_count, top = node_ids.shape
    pick = gate_weights.shape[1]
    chunks, _, chunk = down_v.shape
    peers = (nodes // 2) * locals_
    node = lax.axis_index("node")
    local = lax.axis_index("local")
    core = lax.rem(node, 2)
    my_peer = (node // 2) * locals_ + local

    def peer_id(peer, parity):
        return {"node": 2 * (peer // locals_) + parity, "local": lax.rem(peer, locals_)}

    def place(peer, parity):
        return (2 * (peer // locals_) + parity) * locals_ + lax.rem(peer, locals_)

    sibling = {"node": node + 1 - 2 * core, "local": local}

    blocks = s_gate.shape[1] // LANES
    share = nodes // blocks
    block_start = pl.multiple_of((node // share) * LANES, LANES)
    loads = []
    for e in range(experts):
        loads.append(pltpu.make_async_copy(w_gate.at[e], gate_v.at[e], gate_sem.at[e]))
        loads.append(pltpu.make_async_copy(w_up.at[e], up_v.at[e], up_sem.at[e]))
    sg_load = pltpu.make_async_copy(s_gate.at[:, pl.ds(block_start, LANES)], sgate_v, sg_sem)
    su_load = pltpu.make_async_copy(s_up.at[:, pl.ds(block_start, LANES)], sup_v, su_sem)
    loads += [sg_load, su_load]
    down_loads = []
    for c in range(chunks):
        cols = pl.ds(c * chunk, chunk)
        group = [
            pltpu.make_async_copy(
                w_down.at[e, :, cols],
                down_v.at[c, pl.ds(e * units, units), :],
                down_sem.at[c, e],
            )
            for e in range(experts)
        ]
        group.append(
            pltpu.make_async_copy(
                s_down.at[pl.ds(block_start, LANES), cols],
                down_v.at[c, pl.ds(experts * units, LANES), :],
                down_sem.at[c, experts],
            )
        )
        down_loads.append(group)
        loads += group
    for load in loads:
        load.start()

    barrier = pltpu.get_barrier_semaphore()
    pl.semaphore_signal(barrier, inc=1, device_id=sibling, device_id_type=MESH)

    def greet(step, carry):
        peer = lax.rem(my_peer + step, peers)
        pl.semaphore_signal(barrier, inc=1, device_id=peer_id(peer, core), device_id_type=MESH)
        return carry

    lax.fori_loop(1, peers, greet, 0)

    packed[:, :width] = tokens[...]
    lanes = packed.shape[1] - width
    lane = lax.broadcasted_iota(jnp.int32, (row_count, lanes), 1)
    row_at = lax.broadcasted_iota(jnp.int32, (row_count, top), 0)
    own_gates = jnp.zeros((row_count, lanes), jnp.float32)
    for p in range(pick):
        key = node_ids[...] * experts + expert_order[p]
        weights = jnp.zeros((row_count, top), jnp.float32)
        for t in range(row_count):
            weights = jnp.where(row_at == t, gate_weights[t].astype(jnp.float32)[p : p + 1], weights)
        for k in range(top):
            own_gates = own_gates + jnp.where(
                lane == key[:, k : k + 1], weights[:, k : k + 1], 0.0
            )
    packed[:, width:] = own_gates.astype(jnp.bfloat16)
    pl.semaphore_wait(barrier, peers)

    def gather_copy(step):
        return pltpu.make_async_remote_copy(
            src_ref=packed,
            dst_ref=gathered.at[place(my_peer, core)],
            send_sem=g_send.at[step],
            recv_sem=g_recv.at[step],
            device_id=peer_id(lax.rem(my_peer + step, peers), core),
            device_id_type=MESH,
        )

    def forward_copy(step):
        where = place(lax.rem(my_peer - step + peers, peers), core)
        return pltpu.make_async_remote_copy(
            src_ref=gathered.at[where],
            dst_ref=gathered.at[where],
            send_sem=f_send.at[step],
            recv_sem=f_recv.at[step],
            device_id=sibling,
            device_id_type=MESH,
        )

    own_forward = pltpu.make_async_remote_copy(
        src_ref=packed,
        dst_ref=gathered.at[place(my_peer, core)],
        send_sem=f_send.at[0],
        recv_sem=f_recv.at[0],
        device_id=sibling,
        device_id_type=MESH,
    )

    def start_gather(step, carry):
        gather_copy(step).start()
        return carry

    lax.fori_loop(1, peers, start_gather, 0)
    own_forward.start()
    gathered[place(my_peer, core)] = packed[...]

    def pass_on(step, carry):
        gather_copy(step).wait_recv()
        forward_copy(step).start()
        return carry

    lax.fori_loop(1, peers, pass_on, 0)

    def arrived(step, carry):
        forward_copy(step).wait_recv()
        return carry

    lax.fori_loop(0, peers, arrived, 0)
    for i in range(nodes * locals_):
        rows_wide[i * row_count : (i + 1) * row_count, :] = gathered[i].astype(jnp.float32)
    rows[...] = rows_wide[:, :width].astype(jnp.bfloat16)

    gates = rows_wide[:, width:]
    lane = lax.broadcasted_iota(jnp.int32, gates.shape, 1)

    def expert(e, carry):
        pltpu.make_async_copy(w_gate.at[e], gate_v.at[e], gate_sem.at[e]).wait()
        g = jnp.dot(rows[...], gate_v[e], preferred_element_type=jnp.float32)
        pltpu.make_async_copy(w_up.at[e], up_v.at[e], up_sem.at[e]).wait()
        u = jnp.dot(rows[...], up_v[e], preferred_element_type=jnp.float32)
        weight = jnp.sum(jnp.where(lane == node * experts + e, gates, 0.0), axis=1, keepdims=True)
        value = g / (1.0 + jnp.exp(-g)) * u * weight
        hidden[:, pl.ds(pl.multiple_of(e * units, LANES), units)] = value.astype(jnp.bfloat16)
        return carry

    lax.fori_loop(0, experts, expert, 0)
    sg_load.wait()
    g = jnp.dot(rows[...], sgate_v[...], preferred_element_type=jnp.float32)
    su_load.wait()
    u = jnp.dot(rows[...], sup_v[...], preferred_element_type=jnp.float32)
    part = LANES // share
    first = lax.rem(node, share) * part
    unit = lax.broadcasted_iota(jnp.int32, g.shape, 1)
    owned = jnp.logical_and(unit >= first, unit < first + part)
    value = jnp.where(owned, g / (1.0 + jnp.exp(-g)) * u, 0.0)
    hidden[:, experts * units :] = value.astype(jnp.bfloat16)

    def sib_copy(c):
        return pltpu.make_async_remote_copy(
            src_ref=sib_out.at[c],
            dst_ref=sib_in.at[c],
            send_sem=s_send.at[c],
            recv_sem=s_recv.at[c],
            device_id=sibling,
            device_id_type=MESH,
        )

    def piece_copy(c, step):
        peer = lax.rem(my_peer + step, peers)
        return pltpu.make_async_remote_copy(
            src_ref=piece_out.at[c, peer],
            dst_ref=piece_in.at[c, step],
            send_sem=b_send.at[c, step],
            recv_sem=b_recv.at[c, step],
            device_id=peer_id(peer, core),
            device_id_type=MESH,
        )

    span = locals_ * row_count

    def project(c):
        for load in down_loads[c]:
            load.wait()
        total = jnp.dot(hidden[...], down_v[c], preferred_element_type=jnp.float32)
        for z in range(nodes // 2):
            even = total[2 * z * span : (2 * z + 1) * span]
            odd = total[(2 * z + 1) * span : (2 * z + 2) * span]
            mine[c, z * span : (z + 1) * span, :] = jnp.where(core == 0, even, odd)
            sib_out[c, z * span : (z + 1) * span, :] = jnp.where(core == 0, odd, even).astype(
                jnp.bfloat16
            )
        sib_copy(c).start()

    def send_on(c):
        sib_copy(c).wait_recv()
        both = (mine[c] + sib_in[c].astype(jnp.float32)).astype(jnp.bfloat16)
        for peer in range(peers):
            piece_out[c, peer] = both[peer * row_count : (peer + 1) * row_count]

        def start_piece(step, carry):
            piece_copy(c, step).start()
            return carry

        lax.fori_loop(1, peers, start_piece, 0)

    def finish(c):
        def add(step, total):
            piece_copy(c, step).wait_recv()
            return total + piece_in[c, step].astype(jnp.float32)

        total = lax.fori_loop(1, peers, add, piece_out[c, my_peer].astype(jnp.float32))
        out[:, c * chunk : (c + 1) * chunk] = total.astype(out.dtype)

    for c in range(chunks):
        project(c)
        if c >= 1:
            send_on(c - 1)
    send_on(chunks - 1)
    for c in range(chunks):
        finish(c)

    own_forward.wait_send()

    def sent(step, carry):
        gather_copy(step).wait_send()
        forward_copy(step).wait_send()
        for c in range(chunks):
            piece_copy(c, step).wait_send()
        return carry

    lax.fori_loop(1, peers, sent, 0)
    for c in range(chunks):
        sib_copy(c).wait_send()


def per_device(
    nodes,
    locals_,
    tokens,
    node_ids,
    expert_order,
    gate_weights,
    expert_gate,
    expert_up,
    expert_down,
    shared_gate,
    shared_up,
    shared_down,
):
    row_count, width = tokens.shape
    experts, _, units = expert_gate.shape
    gate_lanes = -(-nodes * experts // LANES) * LANES
    order = jnp.transpose(expert_order, (2, 0, 1))
    weights = jnp.transpose(gate_weights, (0, 2, 1))
    full = width + gate_lanes
    devices = nodes * locals_
    peers = devices // 2
    total = devices * row_count
    chunk = width // CHUNKS
    deep = experts * units + LANES
    half = total // 2
    bf, f32 = jnp.bfloat16, jnp.float32
    dma = pltpu.SemaphoreType.DMA
    hbm = pl.BlockSpec(memory_space=pl.ANY)
    vmem = pl.BlockSpec(memory_space=pltpu.VMEM)
    result = pl.pallas_call(
        functools.partial(layer_kernel, nodes, locals_),
        out_shape=jax.ShapeDtypeStruct((row_count, width), f32),
        in_specs=[vmem] * 4 + [hbm] * 6,
        out_specs=vmem,
        scratch_shapes=[
            pltpu.VMEM((experts, width, units), bf),
            pltpu.VMEM((experts, width, units), bf),
            pltpu.VMEM((width, LANES), bf),
            pltpu.VMEM((width, LANES), bf),
            pltpu.VMEM((CHUNKS, deep, chunk), bf),
            pltpu.VMEM((row_count, full), bf),
            pltpu.VMEM((devices, row_count, full), bf),
            pltpu.VMEM((total, full), f32),
            pltpu.VMEM((total, width), bf),
            pltpu.VMEM((total, deep), bf),
            pltpu.VMEM((CHUNKS, half, chunk), bf),
            pltpu.VMEM((CHUNKS, half, chunk), bf),
            pltpu.VMEM((CHUNKS, half, chunk), f32),
            pltpu.VMEM((CHUNKS, peers, row_count, chunk), bf),
            pltpu.VMEM((CHUNKS, peers, row_count, chunk), bf),
            dma((experts,)),
            dma((experts,)),
            dma,
            dma,
            dma((CHUNKS, experts + 1)),
            dma((peers,)),
            dma((peers,)),
            dma((peers,)),
            dma((peers,)),
            dma((CHUNKS,)),
            dma((CHUNKS,)),
            dma((CHUNKS, peers)),
            dma((CHUNKS, peers)),
        ],
        compiler_params=pltpu.CompilerParams(
            collective_id=0, has_side_effects=True, vmem_limit_bytes=60 * 2**20
        ),
        cost_estimate=pl.CostEstimate(
            flops=6 * total * width * deep,
            bytes_accessed=6 * width * deep,
            transcendentals=total * deep,
        ),
    )(
        tokens,
        node_ids,
        order,
        weights,
        expert_gate,
        expert_up,
        expert_down,
        shared_gate,
        shared_up,
        shared_down,
    )
    return result.astype(bf)


def solution(mesh):
    return jax.shard_map(
        functools.partial(per_device, mesh.shape["node"], mesh.shape["local"]),
        mesh=mesh,
        in_specs=(
            P(("groups", "node", "local"), None),
            P(("groups", "node", "local"), None),
            P(("groups", "node", "local"), None, None),
            P(("groups", "node", "local"), None, None),
            P("node", None, "local"),
            P("node", None, "local"),
            P("node", "local", None),
            P(None, "local"),
            P(None, "local"),
            P("local", None),
        ),
        out_specs=P(("groups", "node", "local"), None),
        check_vma=False,
    )
```
